32 devices in a mesh: groups: 2 (over y), vocab: 16 (over z, x, core).
Axes of the slice: x: 2, y: 2, z: 4, core: 2. Of those that a mesh axis runs over, the one named last changes fastest.
Arguments:
- hidden: bfloat16 [512, 4608], P(('groups', 'vocab')), parts along dimension 0, may hold values from -6 to 6
- weight: bfloat16 [8192, 4608], P('vocab'), may hold values from -0.1875 to 0.1875
- log_totals: float32 [512], P('groups'), parts along dimension 0, may hold values from 4 to 6
- token_cotangent: float32 [512], P('groups'), parts along dimension 0, may hold values from 0.25 to 2
- targets: int32 [512], P('groups'), parts along dimension 0, may hold values from 0 to 8191
- block_list: int32 [128, 2], P(('groups', 'vocab')), parts along dimension 0, may hold values from 0 to 1, as said below
- block_valid: int32 [128], P(('groups', 'vocab')), parts along dimension 0, may hold values from 0 to 1, as said below
Outputs:
- grad_hidden: bfloat16 [512, 4608], P(('groups', 'vocab')), parts along dimension 0
- grad_weight: bfloat16 [16384, 4608], P(('groups', 'vocab')), parts along dimension 0
The draws below stay inside these ranges and needn't reach their ends.
There are 2 independent parts, one for each index of `groups`. The reference program is written for one: setup_inputs(seed, part) draws one part's arguments, and reference() takes and returns one part's arrays. A program takes and returns all parts, laid end to end along the dimension named above; an argument that names none is the same for every part. Nothing has to cross between parts.
Inputs may be any that keep to these rules, and one draw needn't show every extreme that they name: `block_list`: entries s * 4 to s * 4 + 3 belong to vocabulary shard s. Column 0 is a token block below 2, column 1 a vocabulary block below 2; the pairs of one shard are all distinct. `block_valid`: the used entries of a shard come first; every shard uses at least one, and at least one shard uses all 4.
All inputs are finite; a program needn't handle non-finite values.
Results may differ from the reference program's by a relative error of at most 0.0067.
Values may be sent and summed in bfloat16 or wider, within the bound.
A program may use at most 128 MiB of HBM per device.

```python
import math
import jax
import jax.numpy as jnp
from jax import lax

D = 4608
V_DEV = 512
TB = 128
VB = 256
MAXB = 4
TOKENS = 256
VOCAB = 8192
VBLOCKS = 2
ENTRIES = 64
N_VOCAB = 16


def plan_lists(key):
    shard_count = ENTRIES // MAXB
    pair_count = TOKENS // TB * VBLOCKS
    subkeys = jax.random.split(key, 5)
    light_counts = jax.random.randint(subkeys[0], (shard_count,), 1, 3)
    heavy_counts = jax.random.randint(subkeys[1], (shard_count,), MAXB // 2, MAXB + 1)
    chosen = jax.random.randint(subkeys[2], (shard_count,), 0, 8) == 0
    counts = jnp.where(chosen, heavy_counts, light_counts)
    fullest = jax.random.randint(subkeys[3], (), 0, shard_count)
    counts = jnp.where(jnp.arange(shard_count) == fullest, MAXB, counts)
    scores = jax.random.randint(subkeys[4], (shard_count, pair_count), 0, 1 << 20) * pair_count + jnp.arange(pair_count)[None, :]
    ranked = jnp.argsort(scores, axis=1)[:, :MAXB].astype(jnp.int32)
    return (counts.astype(jnp.int32), ranked)


def draw_block_list(key, part):
    counts, ranked = plan_lists(key)
    paired = jnp.stack([ranked // VBLOCKS, ranked % VBLOCKS], axis=-1)
    return paired.reshape(ENTRIES, 2).astype(jnp.int32)


def draw_block_valid(key, part):
    counts, ranked = plan_lists(key)
    places = jnp.arange(MAXB)[None, :]
    return (places < counts[:, None]).astype(jnp.int32).reshape(ENTRIES)


def place_ends(drawn, key, low, high):
    longest = drawn.shape.index(max(drawn.shape))
    spots = []
    for shift in (0, 1):
        where = [jax.random.randint(jax.random.fold_in(key, axis), (), 0, length) for axis, length in enumerate(drawn.shape)]
        where[longest] = (where[longest] + shift) % drawn.shape[longest]
        spots.append(tuple(where))
    return drawn.at[spots[0]].set(low).at[spots[1]].set(high)


def steps_of(stream_key, dims, cuts, low, top_value):
    gain, own = 1.0, jax.random.fold_in(stream_key, 6)
    for dim, blocks in cuts:
        heights = jnp.exp(jax.random.uniform(jax.random.fold_in(own, dim), (blocks,), jnp.float32, low / len(cuts), top_value / len(cuts)))
        gain = gain * jnp.repeat(heights, dims[dim] // blocks).reshape([-1 if axis == dim else 1 for axis in range(len(dims))])
    return gain


def scatter_about(own_key, extent, width, bound, pieces=(), held_as=jnp.bfloat16):
    level = steps_of(own_key, extent, pieces, -0.22, 0.18) if pieces else 1.0
    values = jax.random.normal(own_key, extent, jnp.float32) * width * level
    return jnp.minimum(jnp.maximum(values, -bound), bound).astype(held_as)


def setup_inputs(seed: int = 0, part: int = 0) -> dict:
    key_of = jax.random.split(jax.random.key(seed), 8)
    own_keys = jax.random.split(jax.random.fold_in(key_of[7], part), 8)
    return {
        "hidden": scatter_about(own_keys[0], (TOKENS, D), 1.0, 6.0, ((0, 16),)),
        "weight": scatter_about(key_of[1], (VOCAB, D), (D // 4) ** -0.5, 0.1875, ((0, 16),)),
        "log_totals": jnp.clip(jax.random.uniform(own_keys[2], (TOKENS,), jnp.float32, 4.0, 6.0), 4.0, 6.0),
        "token_cotangent": jnp.clip(jnp.exp(jax.random.uniform(own_keys[3], (TOKENS,), jnp.float32, math.log(0.25), math.log(2.0))), 0.25, 2.0),
        "targets": place_ends(jax.random.randint(own_keys[4], (TOKENS,), 0, VOCAB), jax.random.fold_in(own_keys[4], 1), 0, VOCAB - 1).astype(jnp.int32),
        "block_list": draw_block_list(jax.random.fold_in(jax.random.fold_in(key_of[7], part), 71), part),
        "block_valid": draw_block_valid(jax.random.fold_in(jax.random.fold_in(key_of[7], part), 71), part),
    }


def take_rows(source, start, count):
    return lax.dynamic_slice_in_dim(source, start, count, 0)


def add_rows(target, start, term):
    current = lax.dynamic_slice_in_dim(target, start, term.shape[0], 0)
    return lax.dynamic_update_slice_in_dim(target, current + term, start, 0)


def block_gradient(rows_hidden, columns, totals, cotangent, labels, first_column):
    logits = jnp.dot(rows_hidden, columns.T, preferred_element_type=jnp.float32)
    column_ids = first_column + lax.broadcasted_iota(jnp.int32, (1, columns.shape[0]), 1)
    target_hit = (labels[:, None] == column_ids).astype(jnp.float32)
    return (cotangent[:, None] * (jnp.exp(logits - totals[:, None]) - target_hit)).astype(jnp.bfloat16)


def reference(hidden, weight, log_totals, token_cotangent, targets, block_list, block_valid):
    weight_shards = weight.reshape(N_VOCAB, V_DEV, D)
    shard_lists = block_list.reshape(N_VOCAB, MAXB, 2)
    shard_flags = block_valid.reshape(N_VOCAB, MAXB)
    shard_ids = jnp.arange(N_VOCAB, dtype=jnp.int32)

    def shard_step(row_sums, inputs):
        shard_weight, entries, valid_flags, shard_id = inputs

        def one_entry(position, carry):
            def compute_entry(carried):
                row_acc, column_acc = carried
                token_start = entries[position, 0] * TB
                vocab_start = entries[position, 1] * VB
                rows_hidden = take_rows(hidden, token_start, TB)
                columns = take_rows(shard_weight, vocab_start, VB)
                gradient = block_gradient(rows_hidden, columns, take_rows(log_totals, token_start, TB),
                                          take_rows(token_cotangent, token_start, TB),
                                          take_rows(targets, token_start, TB), shard_id * V_DEV + vocab_start)
                row_acc = add_rows(row_acc, token_start, jnp.dot(gradient, columns, preferred_element_type=jnp.float32))
                column_acc = add_rows(column_acc, vocab_start, jnp.dot(gradient.T, rows_hidden, preferred_element_type=jnp.float32))
                return row_acc, column_acc
            return lax.cond(valid_flags[position] > 0, compute_entry, lambda carried: carried, carry)

        row_sums, column_sums = lax.fori_loop(0, MAXB, one_entry, (row_sums, jnp.zeros((V_DEV, D), jnp.float32)))
        return row_sums, column_sums.astype(jnp.bfloat16)

    row_sums, grad_columns = lax.scan(shard_step, jnp.zeros((TOKENS, D), jnp.float32),
                                      (weight_shards, shard_lists, shard_flags, shard_ids))
    return row_sums.astype(jnp.bfloat16), grad_columns.reshape(VOCAB, D)
```

```python
import jax
import jax.numpy as jnp
from jax import lax
from jax.experimental import pallas as pl
from jax.experimental.pallas import tpu as pltpu
from jax.sharding import PartitionSpec as P

TB = 128
VB = 256


def take_rows(source, start, count):
    return lax.dynamic_slice_in_dim(source, start, count, 0)


def add_rows(target, start, term):
    current = lax.dynamic_slice_in_dim(target, start, term.shape[0], 0)
    return lax.dynamic_update_slice_in_dim(target, current + term, start, 0)


def block_gradient(rows_hidden, columns, totals, cotangent, labels, first_column):
    logits = jnp.dot(rows_hidden, columns.T, preferred_element_type=jnp.float32)
    column_ids = first_column + lax.broadcasted_iota(jnp.int32, (1, columns.shape[0]), 1)
    target_hit = (labels[:, None] == column_ids).astype(jnp.float32)
    return (cotangent[:, None] * (jnp.exp(logits - totals[:, None]) - target_hit)).astype(
        jnp.bfloat16
    )


def local(hidden, weight, log_totals, token_cotangent, targets, block_list, block_valid):
    gathered = lax.all_gather(hidden, "vocab", axis=0, tiled=True)
    my_index = lax.axis_index("vocab")
    vocab_rows = weight.shape[0]
    tokens = gathered.shape[0]
    features = gathered.shape[1]
    entries = block_list.shape[0]
    first_own = my_index * vocab_rows
    token_index = block_list[:, 0]
    vocab_index = block_list[:, 1]
    grad_rows = jnp.zeros((tokens, features), jnp.float32)
    grad_cols = jnp.zeros((vocab_rows, features), jnp.float32)
    keep_entry = block_valid > 0

    def own_entry(position, carry):

        def compute_entry(carried):
            row_acc, column_acc = carried
            token_start = token_index[position] * TB
            vocab_start = vocab_index[position] * VB
            rows_hidden = take_rows(gathered, token_start, TB)
            columns = take_rows(weight, vocab_start, VB)
            gradient = block_gradient(
                rows_hidden,
                columns,
                take_rows(log_totals, token_start, TB),
                take_rows(token_cotangent, token_start, TB),
                take_rows(targets, token_start, TB),
                first_own + vocab_start,
            )
            column_acc = add_rows(
                column_acc,
                vocab_start,
                jnp.dot(gradient.T, rows_hidden, preferred_element_type=jnp.float32),
            )
            return (row_acc, column_acc)

        return lax.cond(keep_entry[position], compute_entry, lambda carried: carried, carry)

    grad_rows, grad_cols = lax.fori_loop(0, entries, own_entry, (grad_rows, grad_cols))
    start = jnp.int32(0)
    count = lax.axis_size("vocab") * hidden.shape[0]
    sub_hidden = take_rows(gathered, start, count)
    sub_totals = take_rows(log_totals, start, count)
    sub_weights = take_rows(token_cotangent, start, count)
    sub_labels = take_rows(targets, start, count)
    row_block = lax.broadcasted_iota(jnp.int32, (count, 1), 0) // TB

    def entry_rows(position, running):
        token_block = token_index[position]
        meets = (
            keep_entry[position]
            & (token_block * TB < start + count)
            & (token_block * TB + TB > start)
        )

        def compute_rows(carried):
            vocab_start = vocab_index[position] * VB
            columns = take_rows(weight, vocab_start, VB)
            gradient = block_gradient(
                sub_hidden, columns, sub_totals, sub_weights, sub_labels, first_own + vocab_start
            )
            gradient = jnp.where(row_block == token_block, gradient, jnp.zeros_like(gradient))
            return carried + jnp.dot(gradient, columns, preferred_element_type=jnp.float32)

        return lax.cond(meets, compute_rows, lambda carried: carried, running)

    grad_part = lax.psum_scatter(
        lax.fori_loop(0, entries, entry_rows, take_rows(grad_rows, start, count)),
        "vocab",
        scatter_dimension=0,
        tiled=True,
    )
    return (grad_part.astype(jnp.bfloat16), grad_cols.astype(jnp.bfloat16))


NZ, NX, NC = 4, 2, 2
CHUNK = 16
GROUP = NX * NC * CHUNK
HALVES = 2
GATHER_ORDER = (0, 1, 3, 2)
SCATTER_ORDER = (2, 1, 3, 0)
MESH = pl.DeviceIdType.MESH


def head_kernel(
    hidden, weight, totals, cotangent, labels, entry_list, entry_valid,
    grad_hidden, gradient_out, gathered_out,
    rows, head, grad, part, totals_col, cotangent_col, labels_col,
    core_out, core_in, core_own, x_out, x_in, x_own, z_out, z_in,
    gz_send, gz_recv, gx_send, gx_recv, gc_send, gc_recv,
    sc_send, sc_recv, sx_send, sx_recv, sz_send, sz_recv, local_sem,
):
    me = lax.axis_index("vocab")
    core = lax.rem(me, NC)
    x = lax.rem(me // NC, NX)
    z = me // (NX * NC)
    vocab_rows, features = head.shape
    width = features // HALVES

    def index(z_, x_, c_):
        return z_ * (NX * NC) + x_ * NC + c_

    def plane(k):
        return lax.rem(z + k, NZ)

    def chunk(device):
        return pl.ds(pl.multiple_of(device * CHUNK, CHUNK), CHUNK)

    def piece(offset):
        return pl.ds(pl.multiple_of(offset, CHUNK), CHUNK)

    def remote(source, target, send, recv, device):
        return pltpu.make_async_remote_copy(
            src_ref=source, dst_ref=target, send_sem=send, recv_sem=recv,
            device_id={"vocab": device}, device_id_type=MESH,
        )

    core_peer = index(z, x, 1 - core)
    x_peer = index(z, 1 - x, core)
    z_peers = [index(plane(k), x, core) for k in range(1, NZ)]

    load_head = pltpu.make_async_copy(weight, head, local_sem.at[0])
    load_rows = pltpu.make_async_copy(hidden, rows.at[chunk(me)], local_sem.at[1])
    load_rows.start()
    load_head.start()

    barrier = pltpu.get_barrier_semaphore()
    for peer in [core_peer, x_peer] + z_peers:
        pl.semaphore_signal(barrier, inc=1, device_id={"vocab": peer}, device_id_type=MESH)

    for vector, column in (
        (totals, totals_col), (cotangent, cotangent_col), (labels, labels_col)
    ):
        column[...] = jnp.broadcast_to(vector[...], (128, vector.shape[1])).T

    load_rows.wait()
    pl.semaphore_wait(barrier, NZ + 1)

    def gather_copy(source, send, recv, device):
        held = rows.at[chunk(source)]
        return remote(held, held, send, recv, device)

    gather_z = {
        k: gather_copy(me, gz_send.at[k], gz_recv.at[k], index(lax.rem(z + NZ - k, NZ), x, core))
        for k in range(1, NZ)
    }
    gather_x = {
        k: gather_copy(index(plane(k), x, core), gx_send.at[k], gx_recv.at[k], x_peer)
        for k in range(NZ)
    }
    gather_c = {
        (k, i): gather_copy(
            index(plane(k), (x, 1 - x)[i], core), gc_send.at[2 * k + i], gc_recv.at[2 * k + i], core_peer
        )
        for k in range(NZ)
        for i in range(NX)
    }
    gather_x[0].start()
    for k in GATHER_ORDER[1:]:
        gather_z[k].start()
    gather_c[0, 0].start()

    def dlogits(k):
        zk = plane(k)
        span = pl.ds(pl.multiple_of(zk * GROUP, GROUP), GROUP)
        gather_c[k, 0].wait_recv()
        gather_c[k, 1].wait_recv()
        logits = lax.dot_general(
            rows[span, :], head[...], (((1,), (1,)), ((), ())), preferred_element_type=jnp.float32
        )
        column = lax.broadcasted_iota(jnp.int32, (1, vocab_rows), 1)
        token_block = zk * GROUP // TB
        keep = jnp.zeros((1, vocab_rows), jnp.int32)
        for e in range(entry_valid.shape[0]):
            used = jnp.where(
                (entry_list[e, 0] == token_block) & (entry_valid[e] > 0), entry_list[e, 1], -1
            )
            keep = jnp.where(column // VB == used, 1, keep)
        hit = (labels_col[span, 0:1] == me * vocab_rows + column).astype(jnp.float32)
        value = cotangent_col[span, 0:1] * (jnp.exp(logits - totals_col[span, 0:1]) - hit)
        grad[span, :] = jnp.where(keep > 0, value, 0.0).astype(jnp.bfloat16)

    for i, k in enumerate(GATHER_ORDER):
        if k:
            gather_z[k].wait_recv()
            gather_x[k].start()
            gather_c[k, 0].start()
        gather_x[k].wait_recv()
        gather_c[k, 1].start()
        if i == 0:
            load_head.wait()
        else:
            dlogits(GATHER_ORDER[i - 1])
    dlogits(GATHER_ORDER[-1])

    save_rows = pltpu.make_async_copy(rows, gathered_out, local_sem.at[2])
    save_grad = pltpu.make_async_copy(grad, gradient_out, local_sem.at[3])
    save_rows.start()
    save_grad.start()

    steps = [(k, h) for k in SCATTER_ORDER for h in range(HALVES)]
    scatter_c = [
        remote(core_out.at[s], core_in.at[s], sc_send.at[s], sc_recv.at[s], core_peer)
        for s in range(len(steps))
    ]
    scatter_x = [
        remote(x_out.at[s], x_in.at[s], sx_send.at[s], sx_recv.at[s], x_peer)
        for s in range(len(steps))
    ]
    scatter_z = {
        s: remote(
            z_out.at[s], z_in.at[s], sz_send.at[s], sz_recv.at[s], index(plane(k), x, core)
        )
        for s, (k, h) in enumerate(steps)
        if k
    }

    def make_part(s):
        k, h = steps[s]
        span = pl.ds(pl.multiple_of(plane(k) * GROUP, GROUP), GROUP)
        part[...] = jnp.dot(
            grad[span, :], head[:, h * width:(h + 1) * width], preferred_element_type=jnp.float32
        )
        for i in range(NX):
            here = slice(i * CHUNK, (i + 1) * CHUNK)
            core_out[s, here, :] = part[piece((i * NC + 1 - core) * CHUNK), :].astype(jnp.bfloat16)
            core_own[s, here, :] = part[piece((i * NC + core) * CHUNK), :]
        scatter_c[s].start()

    def add_core(s):
        scatter_c[s].wait_recv()
        away, own = piece((1 - x) * CHUNK), piece(x * CHUNK)
        x_out[s] = (core_own[s, away, :] + core_in[s, away, :].astype(jnp.float32)).astype(jnp.bfloat16)
        scatter_x[s].start()
        x_own[s] = core_own[s, own, :] + core_in[s, own, :].astype(jnp.float32)

    def add_x(s):
        scatter_x[s].wait_recv()
        total = x_own[s] + x_in[s].astype(jnp.float32)
        if s in scatter_z:
            z_out[s] = total.astype(jnp.bfloat16)
            scatter_z[s].start()
        else:
            x_own[s] = total

    for s in range(len(steps) + 2):
        if s < len(steps):
            make_part(s)
        if 0 <= s - 1 < len(steps):
            add_core(s - 1)
        if 0 <= s - 2 < len(steps):
            add_x(s - 2)

    for h in range(HALVES):
        total = x_own[steps.index((0, h))]
        for s, (k, half) in enumerate(steps):
            if k and half == h:
                scatter_z[s].wait_recv()
                total = total + z_in[s].astype(jnp.float32)
        grad_hidden[:, h * width:(h + 1) * width] = total.astype(jnp.bfloat16)

    for copy in (
        list(gather_z.values()) + list(gather_x.values()) + list(gather_c.values())
        + scatter_c + scatter_x + list(scatter_z.values())
    ):
        copy.wait_send()
    save_rows.wait()
    save_grad.wait()


def local_fused(hidden, weight, log_totals, token_cotangent, targets, block_list, block_valid):
    tokens = log_totals.shape[0]
    vocab_rows, features = weight.shape
    width = features // HALVES
    steps = NZ * HALVES
    bf16, f32 = jnp.bfloat16, jnp.float32
    vmem = pl.BlockSpec(memory_space=pltpu.VMEM)
    smem = pl.BlockSpec(memory_space=pltpu.SMEM)
    hbm = pl.BlockSpec(memory_space=pl.ANY)
    dma = pltpu.SemaphoreType.DMA
    grad_hidden, gradient, gathered = pl.pallas_call(
        head_kernel,
        out_shape=(
            jax.ShapeDtypeStruct(hidden.shape, bf16),
            jax.ShapeDtypeStruct((tokens, vocab_rows), bf16),
            jax.ShapeDtypeStruct((tokens, features), bf16),
        ),
        in_specs=[hbm, hbm, vmem, vmem, vmem, smem, smem],
        out_specs=(vmem, hbm, hbm),
        scratch_shapes=[
            pltpu.VMEM((tokens, features), bf16),
            pltpu.VMEM((vocab_rows, features), bf16),
            pltpu.VMEM((tokens, vocab_rows), bf16),
            pltpu.VMEM((GROUP, width), f32),
            pltpu.VMEM((tokens, 128), f32),
            pltpu.VMEM((tokens, 128), f32),
            pltpu.VMEM((tokens, 128), jnp.int32),
            pltpu.VMEM((steps, NX * CHUNK, width), bf16),
            pltpu.VMEM((steps, NX * CHUNK, width), bf16),
            pltpu.VMEM((steps, NX * CHUNK, width), f32),
            pltpu.VMEM((steps, CHUNK, width), bf16),
            pltpu.VMEM((steps, CHUNK, width), bf16),
            pltpu.VMEM((steps, CHUNK, width), f32),
            pltpu.VMEM((steps, CHUNK, width), bf16),
            pltpu.VMEM((steps, CHUNK, width), bf16),
            dma((NZ,)), dma((NZ,)), dma((NZ,)), dma((NZ,)), dma((2 * NZ,)), dma((2 * NZ,)),
            dma((steps,)), dma((steps,)), dma((steps,)), dma((steps,)), dma((steps,)), dma((steps,)),
            dma((4,)),
        ],
        compiler_params=pltpu.CompilerParams(
            collective_id=0, has_side_effects=True, vmem_limit_bytes=48 * 1024 * 1024
        ),
    )(
        hidden, weight, log_totals[None, :], token_cotangent[None, :], targets[None, :],
        block_list, block_valid,
    )
    grad_weight = lax.dot_general(
        gradient, gathered, (((0,), (0,)), ((), ())), preferred_element_type=f32
    )
    return (grad_hidden, grad_weight.astype(bf16))


def solution(mesh):
    placed = (
        P(("groups", "vocab"), None),
        P("vocab", None),
        P("groups"),
        P("groups"),
        P("groups"),
        P(("groups", "vocab"), None),
        P(("groups", "vocab")),
    )
    fused = mesh.shape["vocab"] == NZ * NX * NC
    return jax.shard_map(
        local_fused if fused else local,
        mesh=mesh,
        in_specs=placed,
        out_specs=(P(("groups", "vocab"), None), P(("groups", "vocab"), None)),
        check_vma=False,
    )
```

```python
import jax
import jax.numpy as jnp
from jax import lax
from jax.experimental import pallas as pl
from jax.experimental.pallas import tpu as pltpu
from jax.sharding import PartitionSpec as P

TB = 128
VB = 256


def take_rows(source, start, count):
    return lax.dynamic_slice_in_dim(source, start, count, 0)


def add_rows(target, start, term):
    current = lax.dynamic_slice_in_dim(target, start, term.shape[0], 0)
    return lax.dynamic_update_slice_in_dim(target, current + term, start, 0)


def block_gradient(rows_hidden, columns, totals, cotangent, labels, first_column):
    logits = jnp.dot(rows_hidden, columns.T, preferred_element_type=jnp.float32)
    column_ids = first_column + lax.broadcasted_iota(jnp.int32, (1, columns.shape[0]), 1)
    target_hit = (labels[:, None] == column_ids).astype(jnp.float32)
    return (cotangent[:, None] * (jnp.exp(logits - totals[:, None]) - target_hit)).astype(
        jnp.bfloat16
    )


def local(hidden, weight, log_totals, token_cotangent, targets, block_list, block_valid):
    gathered = lax.all_gather(hidden, "vocab", axis=0, tiled=True)
    my_index = lax.axis_index("vocab")
    vocab_rows = weight.shape[0]
    tokens = gathered.shape[0]
    features = gathered.shape[1]
    entries = block_list.shape[0]
    first_own = my_index * vocab_rows
    token_index = block_list[:, 0]
    vocab_index = block_list[:, 1]
    grad_rows = jnp.zeros((tokens, features), jnp.float32)
    grad_cols = jnp.zeros((vocab_rows, features), jnp.float32)
    keep_entry = block_valid > 0

    def own_entry(position, carry):

        def compute_entry(carried):
            row_acc, column_acc = carried
            token_start = token_index[position] * TB
            vocab_start = vocab_index[position] * VB
            rows_hidden = take_rows(gathered, token_start, TB)
            columns = take_rows(weight, vocab_start, VB)
            gradient = block_gradient(
                rows_hidden,
                columns,
                take_rows(log_totals, token_start, TB),
                take_rows(token_cotangent, token_start, TB),
                take_rows(targets, token_start, TB),
                first_own + vocab_start,
            )
            column_acc = add_rows(
                column_acc,
                vocab_start,
                jnp.dot(gradient.T, rows_hidden, preferred_element_type=jnp.float32),
            )
            return (row_acc, column_acc)

        return lax.cond(keep_entry[position], compute_entry, lambda carried: carried, carry)

    grad_rows, grad_cols = lax.fori_loop(0, entries, own_entry, (grad_rows, grad_cols))
    start = jnp.int32(0)
    count = lax.axis_size("vocab") * hidden.shape[0]
    sub_hidden = take_rows(gathered, start, count)
    sub_totals = take_rows(log_totals, start, count)
    sub_weights = take_rows(token_cotangent, start, count)
    sub_labels = take_rows(targets, start, count)
    row_block = lax.broadcasted_iota(jnp.int32, (count, 1), 0) // TB

    def entry_rows(position, running):
        token_block = token_index[position]
        meets = (
            keep_entry[position]
            & (token_block * TB < start + count)
            & (token_block * TB + TB > start)
        )

        def compute_rows(carried):
            vocab_start = vocab_index[position] * VB
            columns = take_rows(weight, vocab_start, VB)
            gradient = block_gradient(
                sub_hidden, columns, sub_totals, sub_weights, sub_labels, first_own + vocab_start
            )
            gradient = jnp.where(row_block == token_block, gradient, jnp.zeros_like(gradient))
            return carried + jnp.dot(gradient, columns, preferred_element_type=jnp.float32)

        return lax.cond(meets, compute_rows, lambda carried: carried, running)

    grad_part = lax.psum_scatter(
        lax.fori_loop(0, entries, entry_rows, take_rows(grad_rows, start, count)),
        "vocab",
        scatter_dimension=0,
        tiled=True,
    )
    return (grad_part.astype(jnp.bfloat16), grad_cols.astype(jnp.bfloat16))


NZ, NX, NC = 4, 2, 2
CHUNK = 16
GROUP = NX * NC * CHUNK
HALVES = 2
GATHER_HALVES = 2
ARRIVALS = ((0, 1, 2, 3), (1, 2, 0, 3), (2, 1, 3, 0), (3, 2, 1, 0))
SCATTER_ORDER = (1, 3, 2, 0)
MESH = pl.DeviceIdType.MESH


def head_kernel(
    hidden, weight, totals, cotangent, labels, entry_list, entry_valid,
    grad_hidden, gradient_out, gathered_out,
    rows, head, grad, part, totals_row, cotangent_row, labels_row, list_held, valid_held,
    totals_col, cotangent_col, labels_col, logits_acc,
    core_out, core_in, core_own, x_out, x_in, x_own, z_out, z_in,
    gz_send, gz_recv, gx_send, gx_recv, gc_send, gc_recv,
    sc_send, sc_recv, sx_send, sx_recv, sz_send, sz_recv, local_sem,
):
    me = lax.axis_index("vocab")
    core = lax.rem(me, NC)
    x = lax.rem(me // NC, NX)
    z = me // (NX * NC)
    vocab_rows, features = head.shape
    width = features // HALVES
    gather_width = features // GATHER_HALVES

    def index(z_, x_, c_):
        return z_ * (NX * NC) + x_ * NC + c_

    def arrival(j):
        found = jnp.int32(ARRIVALS[0][j])
        for i in range(1, NZ):
            found = jnp.where(z == i, ARRIVALS[i][j], found)
        return found

    arrived = [z] + [arrival(j) for j in range(1, NZ)]
    has_below, has_above = z > 0, z < NZ - 1
    below, above = index(z - 1, x, core), index(z + 1, x, core)

    def piece(offset):
        return pl.ds(pl.multiple_of(offset, CHUNK), CHUNK)

    def remote(source, target, send, recv, device):
        return pltpu.make_async_remote_copy(
            src_ref=source, dst_ref=target, send_sem=send, recv_sem=recv,
            device_id={"vocab": device}, device_id_type=MESH,
        )

    core_peer = index(z, x, 1 - core)
    x_peer = index(z, 1 - x, core)

    load_rows = pltpu.make_async_copy(hidden, rows.at[piece(me * CHUNK)], local_sem.at[0])
    load_head = pltpu.make_async_copy(weight, head, local_sem.at[1])
    small = [
        pltpu.make_async_copy(source, target, local_sem.at[2 + i])
        for i, (source, target) in enumerate((
            (totals, totals_row), (cotangent, cotangent_row), (labels, labels_row),
            (entry_list, list_held), (entry_valid, valid_held),
        ))
    ]
    load_rows.start()
    for copy in small:
        copy.start()
    load_head.start()

    barrier = pltpu.get_barrier_semaphore()

    def greet(peer):
        pl.semaphore_signal(barrier, inc=1, device_id={"vocab": peer}, device_id_type=MESH)

    greet(core_peer)
    greet(x_peer)
    pl.when(has_below)(lambda: greet(below))
    pl.when(has_above)(lambda: greet(above))

    load_rows.wait()
    pl.semaphore_wait(
        barrier, 2 + jnp.where(has_below, 1, 0) + jnp.where(has_above, 1, 0)
    )

    def gather_copy(device, h, send, recv, to):
        held = rows.at[piece(device * CHUNK), h * gather_width:(h + 1) * gather_width]
        return remote(held, held, send, recv, to)

    def gather_z(j, h, to, slot):
        source = arrived[j]
        return gather_copy(
            index(source, x, core), h,
            gz_send.at[slot * GATHER_HALVES + h], gz_recv.at[source * GATHER_HALVES + h], to,
        )

    def forward_z(j, h, act):
        if j == 0:
            pl.when(has_below)(lambda: act(gather_z(0, h, below, 0)))
            pl.when(has_above)(lambda: act(gather_z(0, h, above, NZ)))
        else:
            rising = arrived[j] < z
            pl.when(rising & has_above)(lambda: act(gather_z(j, h, above, j)))
            pl.when((arrived[j] > z) & has_below)(lambda: act(gather_z(j, h, below, j)))

    def start(copy):
        copy.start()

    def sent(copy):
        copy.wait_send()

    places = [(j, h) for j in range(NZ) for h in range(GATHER_HALVES)]
    gather_x = {
        (j, h): gather_copy(
            index(arrived[j], x, core), h,
            gx_send.at[j * GATHER_HALVES + h], gx_recv.at[j * GATHER_HALVES + h], x_peer,
        )
        for j, h in places
    }
    gather_c = {
        (j, i, h): gather_copy(
            index(arrived[j], (x, 1 - x)[i], core), h,
            gc_send.at[(j * NX + i) * GATHER_HALVES + h], gc_recv.at[(j * NX + i) * GATHER_HALVES + h],
            core_peer,
        )
        for j, h in places
        for i in range(NX)
    }

    def add_logits(j, h):
        span = pl.ds(pl.multiple_of(arrived[j] * GROUP, GROUP), GROUP)
        here = slice(h * gather_width, (h + 1) * gather_width)
        for i in range(NX):
            gather_c[j, i, h].wait_recv()
        term = lax.dot_general(
            head[:, here], rows[span, here], (((1,), (1,)), ((), ())),
            preferred_element_type=jnp.float32,
        )
        if h:
            logits_acc[...] += term
        else:
            logits_acc[...] = term
        if h == GATHER_HALVES - 1:
            dlogits(j)

    def dlogits(j):
        span = pl.ds(pl.multiple_of(arrived[j] * GROUP, GROUP), GROUP)
        logits = logits_acc[...].T
        column = lax.broadcasted_iota(jnp.int32, (1, vocab_rows), 1)
        token_block = arrived[j] * GROUP // TB
        keep = jnp.zeros((1, vocab_rows), jnp.int32)
        for e in range(valid_held.shape[0]):
            used = jnp.where(
                (list_held[0, e] == token_block) & (valid_held[e] > 0), list_held[1, e], -1
            )
            keep = jnp.where(column // VB == used, 1, keep)
        hit = (labels_col[span, 0:1] == me * vocab_rows + column).astype(jnp.float32)
        value = cotangent_col[span, 0:1] * (jnp.exp(logits - totals_col[span, 0:1]) - hit)
        grad[span, :] = jnp.where(keep > 0, value, 0.0).astype(jnp.bfloat16)

    steps = [(j, h) for j in SCATTER_ORDER for h in range(HALVES)]
    scatter_c = [
        remote(core_out.at[s], core_in.at[s], sc_send.at[s], sc_recv.at[s], core_peer)
        for s in range(len(steps))
    ]
    scatter_x = [
        remote(x_out.at[s], x_in.at[s], sx_send.at[s], sx_recv.at[s], x_peer)
        for s in range(len(steps))
    ]

    def make_part(s):
        j, h = steps[s]
        span = pl.ds(pl.multiple_of(arrived[j] * GROUP, GROUP), GROUP)
        part[...] = jnp.dot(
            grad[span, :], head[:, h * width:(h + 1) * width], preferred_element_type=jnp.float32
        )
        for i in range(NX):
            here = slice(i * CHUNK, (i + 1) * CHUNK)
            core_out[s, here, :] = part[piece((i * NC + 1 - core) * CHUNK), :].astype(jnp.bfloat16)
            core_own[s, here, :] = part[piece((i * NC + core) * CHUNK), :]
        scatter_c[s].start()

    def add_core(s):
        scatter_c[s].wait_recv()
        away, own = piece((1 - x) * CHUNK), piece(x * CHUNK)
        x_out[s] = (core_own[s, away, :] + core_in[s, away, :].astype(jnp.float32)).astype(jnp.bfloat16)
        scatter_x[s].start()
        x_own[s] = core_own[s, own, :] + core_in[s, own, :].astype(jnp.float32)

    def z_slot(owner, falling, h):
        return (owner * 2 + falling) * HALVES + h

    def scatter_z(s, to, falling):
        j, h = steps[s]
        slot = z_slot(arrived[j], falling, h)
        return remote(z_out.at[s], z_in.at[slot], sz_send.at[s], sz_recv.at[slot], to)

    def pass_z(s, act):
        rises = arrived[steps[s][0]] > z
        pl.when(rises)(lambda: act(scatter_z(s, above, 0)))
        pl.when(jnp.logical_not(rises))(lambda: act(scatter_z(s, below, 1)))

    def add_x(s):
        scatter_x[s].wait_recv()
        total = x_own[s] + x_in[s].astype(jnp.float32)
        x_own[s] = total
        if steps[s][0]:
            rises = arrived[steps[s][0]] > z

            @pl.when(jnp.logical_not((rises & has_below) | (jnp.logical_not(rises) & has_above)))
            def _():
                z_out[s] = x_own[s].astype(jnp.bfloat16)
                pass_z(s, start)

    def take_z(s, falling):
        scatter_z(s, x_peer, falling).wait_recv()
        slot = z_slot(arrived[steps[s][0]], falling, steps[s][1])
        x_own[s] += z_in[slot].astype(jnp.float32)

    def add_z(s):
        rises = arrived[steps[s][0]] > z

        @pl.when(rises & has_below)
        def _():
            take_z(s, 0)
            z_out[s] = x_own[s].astype(jnp.bfloat16)
            scatter_z(s, above, 0).start()

        @pl.when(jnp.logical_not(rises) & has_above)
        def _():
            take_z(s, 1)
            z_out[s] = x_own[s].astype(jnp.bfloat16)
            scatter_z(s, below, 1).start()

    for h in range(GATHER_HALVES):
        gather_x[0, h].start()
        forward_z(0, h, start)
    for h in range(GATHER_HALVES):
        gather_c[0, 0, h].start()
    for copy in small:
        copy.wait()
    for vector, column in (
        (totals_row, totals_col), (cotangent_row, cotangent_col), (labels_row, labels_col)
    ):
        column[...] = jnp.broadcast_to(vector[...], (128, vector.shape[1])).T

    def pass_x(j, h):
        gather_x[j, h].wait_recv()
        gather_c[j, 1, h].start()

    waiting = []
    for j, h in places[GATHER_HALVES:]:
        gather_z(j, h, x_peer, j).wait_recv()
        forward_z(j, h, start)
        gather_x[j, h].start()
        gather_c[j, 0, h].start()
        pass_x(j - 1, h)
        if waiting:
            if len(waiting) == 1:
                load_head.wait()
            add_logits(*waiting[-1])
        waiting.append((j - 1, h))
    add_logits(*waiting[-1])
    for s in range(HALVES):
        make_part(s)
    for h in range(GATHER_HALVES):
        pass_x(NZ - 1, h)
        if h:
            add_logits(NZ - 1, h - 1)
    for s in range(HALVES):
        add_core(s)
    add_logits(NZ - 1, GATHER_HALVES - 1)

    save_rows = pltpu.make_async_copy(rows, gathered_out, local_sem.at[7])
    save_grad = pltpu.make_async_copy(grad, gradient_out, local_sem.at[8])

    passing = len(steps) - HALVES
    for s in range(HALVES, len(steps) + 4):
        if s < len(steps):
            make_part(s)
        if HALVES <= s - 1 < len(steps):
            add_core(s - 1)
        if s < 2 * HALVES:
            add_x(s - HALVES)
        if HALVES <= s - 2 < len(steps):
            add_x(s - 2)
        if HALVES <= s - 4 < passing:
            add_z(s - 4)
        if s == len(steps):
            save_rows.start()
            save_grad.start()
    for s in range(HALVES):
        add_z(s)

    for h in range(HALVES):
        s = passing + h
        pl.when(has_below)(lambda: take_z(s, 0))
        pl.when(has_above)(lambda: take_z(s, 1))
        grad_hidden[:, h * width:(h + 1) * width] = x_own[s].astype(jnp.bfloat16)

    for j, h in places:
        forward_z(j, h, sent)
    for copy in list(gather_x.values()) + list(gather_c.values()) + scatter_c + scatter_x:
        copy.wait_send()
    for s in range(passing):
        pass_z(s, sent)
    save_rows.wait()
    save_grad.wait()


def local_fused(hidden, weight, log_totals, token_cotangent, targets, block_list, block_valid):
    tokens = log_totals.shape[0]
    vocab_rows, features = weight.shape
    entries = block_valid.shape[0]
    width = features // HALVES
    steps = NZ * HALVES
    places = NZ * GATHER_HALVES
    bf16, f32, i32 = jnp.bfloat16, jnp.float32, jnp.int32
    hbm = pl.BlockSpec(memory_space=pltpu.HBM)
    dma = pltpu.SemaphoreType.DMA
    grad_hidden, gradient, gathered = pl.pallas_call(
        head_kernel,
        out_shape=(
            jax.ShapeDtypeStruct(hidden.shape, bf16),
            jax.ShapeDtypeStruct((tokens, vocab_rows), bf16),
            jax.ShapeDtypeStruct((tokens, features), bf16),
        ),
        in_specs=[hbm] * 7,
        out_specs=(
            pl.BlockSpec(memory_space=pltpu.VMEM),
            pl.BlockSpec(memory_space=pl.ANY),
            pl.BlockSpec(memory_space=pl.ANY),
        ),
        scratch_shapes=[
            pltpu.VMEM((tokens, features), bf16),
            pltpu.VMEM((vocab_rows, features), bf16),
            pltpu.VMEM((tokens, vocab_rows), bf16),
            pltpu.VMEM((GROUP, width), f32),
            pltpu.VMEM((1, tokens), f32),
            pltpu.VMEM((1, tokens), f32),
            pltpu.VMEM((1, tokens), i32),
            pltpu.SMEM((2, entries), i32),
            pltpu.SMEM((entries,), i32),
            pltpu.VMEM((tokens, 128), f32),
            pltpu.VMEM((tokens, 128), f32),
            pltpu.VMEM((tokens, 128), i32),
            pltpu.VMEM((vocab_rows, GROUP), f32),
            pltpu.VMEM((steps, NX * CHUNK, width), bf16),
            pltpu.VMEM((steps, NX * CHUNK, width), bf16),
            pltpu.VMEM((steps, NX * CHUNK, width), f32),
            pltpu.VMEM((steps, CHUNK, width), bf16),
            pltpu.VMEM((steps, CHUNK, width), bf16),
            pltpu.VMEM((steps, CHUNK, width), f32),
            pltpu.VMEM((steps, CHUNK, width), bf16),
            pltpu.VMEM((2 * steps, CHUNK, width), bf16),
            dma((places + GATHER_HALVES,)), dma((places,)),
            dma((places,)), dma((places,)), dma((2 * places,)), dma((2 * places,)),
            dma((steps,)), dma((steps,)), dma((steps,)), dma((steps,)),
            dma((steps,)), dma((2 * steps,)),
            dma((9,)),
        ],
        compiler_params=pltpu.CompilerParams(
            collective_id=0, has_side_effects=True, vmem_limit_bytes=64 * 1024 * 1024
        ),
    )(
        hidden, weight, log_totals[None, :], token_cotangent[None, :], targets[None, :],
        block_list.T, block_valid,
    )
    grad_weight = lax.dot_general(
        gradient, gathered, (((0,), (0,)), ((), ())), preferred_element_type=f32
    )
    return (grad_hidden, grad_weight.astype(bf16))


def solution(mesh):
    placed = (
        P(("groups", "vocab"), None),
        P("vocab", None),
        P("groups"),
        P("groups"),
        P("groups"),
        P(("groups", "vocab"), None),
        P(("groups", "vocab")),
    )
    fused = mesh.shape["vocab"] == NZ * NX * NC
    return jax.shard_map(
        local_fused if fused else local,
        mesh=mesh,
        in_specs=placed,
        out_specs=(P(("groups", "vocab"), None), P(("groups", "vocab"), None)),
        check_vma=False,
    )
```

```python
import jax
import jax.numpy as jnp
from jax import lax
from jax.experimental import pallas as pl
from jax.experimental.pallas import tpu as pltpu
from jax.sharding import PartitionSpec as P

TB = 128
VB = 256


def take_rows(source, start, count):
    return lax.dynamic_slice_in_dim(source, start, count, 0)


def add_rows(target, start, term):
    current = lax.dynamic_slice_in_dim(target, start, term.shape[0], 0)
    return lax.dynamic_update_slice_in_dim(target, current + term, start, 0)


def block_gradient(rows_hidden, columns, totals, cotangent, labels, first_column):
    logits = jnp.dot(rows_hidden, columns.T, preferred_element_type=jnp.float32)
    column_ids = first_column + lax.broadcasted_iota(jnp.int32, (1, columns.shape[0]), 1)
    target_hit = (labels[:, None] == column_ids).astype(jnp.float32)
    return (cotangent[:, None] * (jnp.exp(logits - totals[:, None]) - target_hit)).astype(
        jnp.bfloat16
    )


def local(hidden, weight, log_totals, token_cotangent, targets, block_list, block_valid):
    gathered = lax.all_gather(hidden, "vocab", axis=0, tiled=True)
    my_index = lax.axis_index("vocab")
    vocab_rows = weight.shape[0]
    tokens = gathered.shape[0]
    features = gathered.shape[1]
    entries = block_list.shape[0]
    first_own = my_index * vocab_rows
    token_index = block_list[:, 0]
    vocab_index = block_list[:, 1]
    grad_rows = jnp.zeros((tokens, features), jnp.float32)
    grad_cols = jnp.zeros((vocab_rows, features), jnp.float32)
    keep_entry = block_valid > 0

    def own_entry(position, carry):

        def compute_entry(carried):
            row_acc, column_acc = carried
            token_start = token_index[position] * TB
            vocab_start = vocab_index[position] * VB
            rows_hidden = take_rows(gathered, token_start, TB)
            columns = take_rows(weight, vocab_start, VB)
            gradient = block_gradient(
                rows_hidden,
                columns,
                take_rows(log_totals, token_start, TB),
                take_rows(token_cotangent, token_start, TB),
                take_rows(targets, token_start, TB),
                first_own + vocab_start,
            )
            column_acc = add_rows(
                column_acc,
                vocab_start,
                jnp.dot(gradient.T, rows_hidden, preferred_element_type=jnp.float32),
            )
            return (row_acc, column_acc)

        return lax.cond(keep_entry[position], compute_entry, lambda carried: carried, carry)

    grad_rows, grad_cols = lax.fori_loop(0, entries, own_entry, (grad_rows, grad_cols))
    start = jnp.int32(0)
    count = lax.axis_size("vocab") * hidden.shape[0]
    sub_hidden = take_rows(gathered, start, count)
    sub_totals = take_rows(log_totals, start, count)
    sub_weights = take_rows(token_cotangent, start, count)
    sub_labels = take_rows(targets, start, count)
    row_block = lax.broadcasted_iota(jnp.int32, (count, 1), 0) // TB

    def entry_rows(position, running):
        token_block = token_index[position]
        meets = (
            keep_entry[position]
            & (token_block * TB < start + count)
            & (token_block * TB + TB > start)
        )

        def compute_rows(carried):
            vocab_start = vocab_index[position] * VB
            columns = take_rows(weight, vocab_start, VB)
            gradient = block_gradient(
                sub_hidden, columns, sub_totals, sub_weights, sub_labels, first_own + vocab_start
            )
            gradient = jnp.where(row_block == token_block, gradient, jnp.zeros_like(gradient))
            return carried + jnp.dot(gradient, columns, preferred_element_type=jnp.float32)

        return lax.cond(meets, compute_rows, lambda carried: carried, running)

    grad_part = lax.psum_scatter(
        lax.fori_loop(0, entries, entry_rows, take_rows(grad_rows, start, count)),
        "vocab",
        scatter_dimension=0,
        tiled=True,
    )
    return (grad_part.astype(jnp.bfloat16), grad_cols.astype(jnp.bfloat16))


NZ, NX, NC = 4, 2, 2
CHUNK = 16
GROUP = NX * NC * CHUNK
HALVES = 2
GATHER_HALVES = 2
ARRIVALS = ((0, 1, 2, 3), (1, 2, 0, 3), (2, 1, 3, 0), (3, 2, 1, 0))
SCATTER_ORDER = (1, 3, 2, 0)
MESH = pl.DeviceIdType.MESH


def head_kernel(
    hidden, weight, totals, cotangent, labels, entry_list, entry_valid,
    grad_hidden, gradient_out, gathered_out,
    rows, head, grad, part, totals_row, cotangent_row, labels_row, list_held, valid_held,
    totals_col, cotangent_col, labels_col, logits_acc,
    core_out, core_in, core_own, x_out, x_in, x_own, z_out, z_in,
    gz_send, gz_recv, gx_send, gx_recv, gc_send, gc_recv,
    sc_send, sc_recv, sx_send, sx_recv, sz_send, sz_recv, local_sem,
):
    me = lax.axis_index("vocab")
    core = lax.rem(me, NC)
    x = lax.rem(me // NC, NX)
    z = me // (NX * NC)
    vocab_rows, features = head.shape
    width = features // HALVES
    gather_width = features // GATHER_HALVES

    def index(z_, x_, c_):
        return z_ * (NX * NC) + x_ * NC + c_

    def arrival(j):
        found = jnp.int32(ARRIVALS[0][j])
        for i in range(1, NZ):
            found = jnp.where(z == i, ARRIVALS[i][j], found)
        return found

    arrived = [z] + [arrival(j) for j in range(1, NZ)]
    has_below, has_above = z > 0, z < NZ - 1
    below, above = index(z - 1, x, core), index(z + 1, x, core)

    def piece(offset):
        return pl.ds(pl.multiple_of(offset, CHUNK), CHUNK)

    def remote(source, target, send, recv, device):
        return pltpu.make_async_remote_copy(
            src_ref=source, dst_ref=target, send_sem=send, recv_sem=recv,
            device_id={"vocab": device}, device_id_type=MESH,
        )

    core_peer = index(z, x, 1 - core)
    x_peer = index(z, 1 - x, core)

    load_rows = pltpu.make_async_copy(hidden, rows.at[piece(me * CHUNK)], local_sem.at[0])
    load_head = pltpu.make_async_copy(weight, head, local_sem.at[1])
    small = [
        pltpu.make_async_copy(source, target, local_sem.at[2 + i])
        for i, (source, target) in enumerate((
            (totals, totals_row), (cotangent, cotangent_row), (labels, labels_row),
            (entry_list, list_held), (entry_valid, valid_held),
        ))
    ]
    load_rows.start()
    for copy in small:
        copy.start()
    load_head.start()

    barrier = pltpu.get_barrier_semaphore()

    def greet(peer):
        pl.semaphore_signal(barrier, inc=1, device_id={"vocab": peer}, device_id_type=MESH)

    greet(core_peer)
    greet(x_peer)
    for k in range(1, NZ):
        greet(index(lax.rem(z + k, NZ), x, core))

    load_rows.wait()
    pl.semaphore_wait(barrier, NZ + 1)

    def gather_copy(device, h, send, recv, to):
        held = rows.at[piece(device * CHUNK), h * gather_width:(h + 1) * gather_width]
        return remote(held, held, send, recv, to)

    def gather_z(j, h, to, slot):
        source = arrived[j]
        return gather_copy(
            index(source, x, core), h,
            gz_send.at[slot * GATHER_HALVES + h], gz_recv.at[source * GATHER_HALVES + h], to,
        )

    def forward_z(j, h, act):
        if j == 0:
            pl.when(has_below)(lambda: act(gather_z(0, h, below, 0)))
            pl.when(has_above)(lambda: act(gather_z(0, h, above, NZ)))
        else:
            rising = arrived[j] < z
            pl.when(rising & has_above)(lambda: act(gather_z(j, h, above, j)))
            pl.when((arrived[j] > z) & has_below)(lambda: act(gather_z(j, h, below, j)))

    def start(copy):
        copy.start()

    def sent(copy):
        copy.wait_send()

    places = [(j, h) for j in range(NZ) for h in range(GATHER_HALVES)]
    gather_x = {
        (j, h): gather_copy(
            index(arrived[j], x, core), h,
            gx_send.at[j * GATHER_HALVES + h], gx_recv.at[j * GATHER_HALVES + h], x_peer,
        )
        for j, h in places
    }
    gather_c = {
        (j, i, h): gather_copy(
            index(arrived[j], (x, 1 - x)[i], core), h,
            gc_send.at[(j * NX + i) * GATHER_HALVES + h], gc_recv.at[(j * NX + i) * GATHER_HALVES + h],
            core_peer,
        )
        for j, h in places
        for i in range(NX)
    }

    def add_logits(j, h):
        span = pl.ds(pl.multiple_of(arrived[j] * GROUP, GROUP), GROUP)
        here = slice(h * gather_width, (h + 1) * gather_width)
        for i in range(NX):
            gather_c[j, i, h].wait_recv()
        term = lax.dot_general(
            head[:, here], rows[span, here], (((1,), (1,)), ((), ())),
            preferred_element_type=jnp.float32,
        )
        if h:
            logits_acc[...] += term
        else:
            logits_acc[...] = term
        if h == GATHER_HALVES - 1:
            dlogits(j)

    def dlogits(j):
        span = pl.ds(pl.multiple_of(arrived[j] * GROUP, GROUP), GROUP)
        logits = logits_acc[...].T
        column = lax.broadcasted_iota(jnp.int32, (1, vocab_rows), 1)
        token_block = arrived[j] * GROUP // TB
        keep = jnp.zeros((1, vocab_rows), jnp.int32)
        for e in range(valid_held.shape[0]):
            used = jnp.where(
                (list_held[0, e] == token_block) & (valid_held[e] > 0), list_held[1, e], -1
            )
            keep = jnp.where(column // VB == used, 1, keep)
        hit = (labels_col[span, 0:1] == me * vocab_rows + column).astype(jnp.float32)
        value = cotangent_col[span, 0:1] * (jnp.exp(logits - totals_col[span, 0:1]) - hit)
        grad[span, :] = jnp.where(keep > 0, value, 0.0).astype(jnp.bfloat16)

    steps = [(j, h) for j in SCATTER_ORDER for h in range(HALVES)]
    scatter_c = [
        remote(core_out.at[s], core_in.at[s], sc_send.at[s], sc_recv.at[s], core_peer)
        for s in range(len(steps))
    ]
    scatter_x = [
        remote(x_out.at[s], x_in.at[s], sx_send.at[s], sx_recv.at[s], x_peer)
        for s in range(len(steps))
    ]

    def make_part(s):
        j, h = steps[s]
        span = pl.ds(pl.multiple_of(arrived[j] * GROUP, GROUP), GROUP)
        part[...] = jnp.dot(
            grad[span, :], head[:, h * width:(h + 1) * width], preferred_element_type=jnp.float32
        )
        for i in range(NX):
            here = slice(i * CHUNK, (i + 1) * CHUNK)
            core_out[s, here, :] = part[piece((i * NC + 1 - core) * CHUNK), :].astype(jnp.bfloat16)
            core_own[s, here, :] = part[piece((i * NC + core) * CHUNK), :]
        scatter_c[s].start()

    def add_core(s):
        scatter_c[s].wait_recv()
        away, own = piece((1 - x) * CHUNK), piece(x * CHUNK)
        x_out[s] = (core_own[s, away, :] + core_in[s, away, :].astype(jnp.float32)).astype(jnp.bfloat16)
        scatter_x[s].start()
        x_own[s] = core_own[s, own, :] + core_in[s, own, :].astype(jnp.float32)

    def scatter_z(s, source):
        j, h = steps[s]
        slot = source * HALVES + h
        return remote(
            z_out.at[s], z_in.at[slot], sz_send.at[s], sz_recv.at[slot],
            index(arrived[j], x, core),
        )

    def add_x(s):
        scatter_x[s].wait_recv()
        total = x_own[s] + x_in[s].astype(jnp.float32)
        if steps[s][0]:
            z_out[s] = total.astype(jnp.bfloat16)
            scatter_z(s, z).start()
        else:
            x_own[s] = total

    for h in range(GATHER_HALVES):
        gather_x[0, h].start()
        forward_z(0, h, start)
    for h in range(GATHER_HALVES):
        gather_c[0, 0, h].start()
    for copy in small:
        copy.wait()
    for vector, column in (
        (totals_row, totals_col), (cotangent_row, cotangent_col), (labels_row, labels_col)
    ):
        column[...] = jnp.broadcast_to(vector[...], (128, vector.shape[1])).T

    def pass_x(j, h):
        gather_x[j, h].wait_recv()
        gather_c[j, 1, h].start()

    waiting = []
    for j, h in places[GATHER_HALVES:]:
        gather_z(j, h, x_peer, j).wait_recv()
        forward_z(j, h, start)
        gather_x[j, h].start()
        gather_c[j, 0, h].start()
        pass_x(j - 1, h)
        if waiting:
            if len(waiting) == 1:
                load_head.wait()
            add_logits(*waiting[-1])
        waiting.append((j - 1, h))
    add_logits(*waiting[-1])
    for s in range(HALVES):
        make_part(s)
    for h in range(GATHER_HALVES):
        pass_x(NZ - 1, h)
        if h:
            add_logits(NZ - 1, h - 1)
    for s in range(HALVES):
        add_core(s)
    add_logits(NZ - 1, GATHER_HALVES - 1)

    save_rows = pltpu.make_async_copy(rows, gathered_out, local_sem.at[7])
    save_grad = pltpu.make_async_copy(grad, gradient_out, local_sem.at[8])

    passing = len(steps) - HALVES
    for s in range(HALVES, len(steps) + 2):
        if s < len(steps):
            make_part(s)
        if HALVES <= s - 1 < len(steps):
            add_core(s - 1)
        if s < 2 * HALVES:
            add_x(s - HALVES)
        if HALVES <= s - 2 < len(steps):
            add_x(s - 2)
        if s == len(steps):
            save_rows.start()
            save_grad.start()

    for h in range(HALVES):
        total = x_own[passing + h]
        for j in range(1, NZ):
            scatter_z(steps.index((j, h)), arrived[j]).wait_recv()
            total = total + z_in[arrived[j] * HALVES + h].astype(jnp.float32)
        grad_hidden[:, h * width:(h + 1) * width] = total.astype(jnp.bfloat16)

    for j, h in places:
        forward_z(j, h, sent)
    for copy in list(gather_x.values()) + list(gather_c.values()) + scatter_c + scatter_x:
        copy.wait_send()
    for s in range(passing):
        scatter_z(s, z).wait_send()
    save_rows.wait()
    save_grad.wait()


def local_fused(hidden, weight, log_totals, token_cotangent, targets, block_list, block_valid):
    tokens = log_totals.shape[0]
    vocab_rows, features = weight.shape
    entries = block_valid.shape[0]
    width = features // HALVES
    steps = NZ * HALVES
    places = NZ * GATHER_HALVES
    bf16, f32, i32 = jnp.bfloat16, jnp.float32, jnp.int32
    hbm = pl.BlockSpec(memory_space=pltpu.HBM)
    dma = pltpu.SemaphoreType.DMA
    grad_hidden, gradient, gathered = pl.pallas_call(
        head_kernel,
        out_shape=(
            jax.ShapeDtypeStruct(hidden.shape, bf16),
            jax.ShapeDtypeStruct((tokens, vocab_rows), bf16),
            jax.ShapeDtypeStruct((tokens, features), bf16),
        ),
        in_specs=[hbm] * 7,
        out_specs=(
            pl.BlockSpec(memory_space=pltpu.VMEM),
            pl.BlockSpec(memory_space=pl.ANY),
            pl.BlockSpec(memory_space=pl.ANY),
        ),
        scratch_shapes=[
            pltpu.VMEM((tokens, features), bf16),
            pltpu.VMEM((vocab_rows, features), bf16),
            pltpu.VMEM((tokens, vocab_rows), bf16),
            pltpu.VMEM((GROUP, width), f32),
            pltpu.VMEM((1, tokens), f32),
            pltpu.VMEM((1, tokens), f32),
            pltpu.VMEM((1, tokens), i32),
            pltpu.SMEM((2, entries), i32),
            pltpu.SMEM((entries,), i32),
            pltpu.VMEM((tokens, 128), f32),
            pltpu.VMEM((tokens, 128), f32),
            pltpu.VMEM((tokens, 128), i32),
            pltpu.VMEM((vocab_rows, GROUP), f32),
            pltpu.VMEM((steps, NX * CHUNK, width), bf16),
            pltpu.VMEM((steps, NX * CHUNK, width), bf16),
            pltpu.VMEM((steps, NX * CHUNK, width), f32),
            pltpu.VMEM((steps, CHUNK, width), bf16),
            pltpu.VMEM((steps, CHUNK, width), bf16),
            pltpu.VMEM((steps, CHUNK, width), f32),
            pltpu.VMEM((steps, CHUNK, width), bf16),
            pltpu.VMEM((steps, CHUNK, width), bf16),
            dma((places + GATHER_HALVES,)), dma((places,)),
            dma((places,)), dma((places,)), dma((2 * places,)), dma((2 * places,)),
            dma((steps,)), dma((steps,)), dma((steps,)), dma((steps,)),
            dma((steps,)), dma((steps,)),
            dma((9,)),
        ],
        compiler_params=pltpu.CompilerParams(
            collective_id=0, has_side_effects=True, vmem_limit_bytes=64 * 1024 * 1024
        ),
    )(
        hidden, weight, log_totals[None, :], token_cotangent[None, :], targets[None, :],
        block_list.T, block_valid,
    )
    grad_weight = lax.dot_general(
        gradient, gathered, (((0,), (0,)), ((), ())), preferred_element_type=f32
    )
    return (grad_hidden, grad_weight.astype(bf16))


def solution(mesh):
    placed = (
        P(("groups", "vocab"), None),
        P("vocab", None),
        P("groups"),
        P("groups"),
        P("groups"),
        P(("groups", "vocab"), None),
        P(("groups", "vocab")),
    )
    fused = mesh.shape["vocab"] == NZ * NX * NC
    return jax.shard_map(
        local_fused if fused else local,
        mesh=mesh,
        in_specs=placed,
        out_specs=(P(("groups", "vocab"), None), P(("groups", "vocab"), None)),
        check_vma=False,
    )
```

```python
import jax
import jax.numpy as jnp
from jax import lax
from jax.experimental import pallas as pl
from jax.experimental.pallas import tpu as pltpu
from jax.sharding import PartitionSpec as P

TB = 128
VB = 256


def take_rows(source, start, count):
    return lax.dynamic_slice_in_dim(source, start, count, 0)


def add_rows(target, start, term):
    current = lax.dynamic_slice_in_dim(target, start, term.shape[0], 0)
    return lax.dynamic_update_slice_in_dim(target, current + term, start, 0)


def block_gradient(rows_hidden, columns, totals, cotangent, labels, first_column):
    logits = jnp.dot(rows_hidden, columns.T, preferred_element_type=jnp.float32)
    column_ids = first_column + lax.broadcasted_iota(jnp.int32, (1, columns.shape[0]), 1)
    target_hit = (labels[:, None] == column_ids).astype(jnp.float32)
    return (cotangent[:, None] * (jnp.exp(logits - totals[:, None]) - target_hit)).astype(
        jnp.bfloat16
    )


def local(hidden, weight, log_totals, token_cotangent, targets, block_list, block_valid):
    gathered = lax.all_gather(hidden, "vocab", axis=0, tiled=True)
    my_index = lax.axis_index("vocab")
    vocab_rows = weight.shape[0]
    tokens = gathered.shape[0]
    features = gathered.shape[1]
    entries = block_list.shape[0]
    first_own = my_index * vocab_rows
    token_index = block_list[:, 0]
    vocab_index = block_list[:, 1]
    grad_rows = jnp.zeros((tokens, features), jnp.float32)
    grad_cols = jnp.zeros((vocab_rows, features), jnp.float32)
    keep_entry = block_valid > 0

    def own_entry(position, carry):

        def compute_entry(carried):
            row_acc, column_acc = carried
            token_start = token_index[position] * TB
            vocab_start = vocab_index[position] * VB
            rows_hidden = take_rows(gathered, token_start, TB)
            columns = take_rows(weight, vocab_start, VB)
            gradient = block_gradient(
                rows_hidden,
                columns,
                take_rows(log_totals, token_start, TB),
                take_rows(token_cotangent, token_start, TB),
                take_rows(targets, token_start, TB),
                first_own + vocab_start,
            )
            column_acc = add_rows(
                column_acc,
                vocab_start,
                jnp.dot(gradient.T, rows_hidden, preferred_element_type=jnp.float32),
            )
            return (row_acc, column_acc)

        return lax.cond(keep_entry[position], compute_entry, lambda carried: carried, carry)

    grad_rows, grad_cols = lax.fori_loop(0, entries, own_entry, (grad_rows, grad_cols))
    start = jnp.int32(0)
    count = lax.axis_size("vocab") * hidden.shape[0]
    sub_hidden = take_rows(gathered, start, count)
    sub_totals = take_rows(log_totals, start, count)
    sub_weights = take_rows(token_cotangent, start, count)
    sub_labels = take_rows(targets, start, count)
    row_block = lax.broadcasted_iota(jnp.int32, (count, 1), 0) // TB

    def entry_rows(position, running):
        token_block = token_index[position]
        meets = (
            keep_entry[position]
            & (token_block * TB < start + count)
            & (token_block * TB + TB > start)
        )

        def compute_rows(carried):
            vocab_start = vocab_index[position] * VB
            columns = take_rows(weight, vocab_start, VB)
            gradient = block_gradient(
                sub_hidden, columns, sub_totals, sub_weights, sub_labels, first_own + vocab_start
            )
            gradient = jnp.where(row_block == token_block, gradient, jnp.zeros_like(gradient))
            return carried + jnp.dot(gradient, columns, preferred_element_type=jnp.float32)

        return lax.cond(meets, compute_rows, lambda carried: carried, running)

    grad_part = lax.psum_scatter(
        lax.fori_loop(0, entries, entry_rows, take_rows(grad_rows, start, count)),
        "vocab",
        scatter_dimension=0,
        tiled=True,
    )
    return (grad_part.astype(jnp.bfloat16), grad_cols.astype(jnp.bfloat16))


NZ, NX, NC = 4, 2, 2
CHUNK = 16
GROUP = NX * NC * CHUNK
HALVES = 2
GATHER_HALVES = 2
ARRIVALS = ((0, 1, 2, 3), (1, 2, 0, 3), (2, 1, 3, 0), (3, 2, 1, 0))
SCATTER_ORDER = (1, 3, 2, 0)
MESH = pl.DeviceIdType.MESH


def head_kernel(
    hidden, weight, totals, cotangent, labels, entry_list, entry_valid,
    grad_hidden, gradient_out, gathered_out,
    rows, head, grad, part, totals_row, cotangent_row, labels_row, list_held, valid_held,
    totals_col, cotangent_col, labels_col, logits_acc,
    core_out, core_in, core_own, x_out, x_in, x_own, z_out, z_in,
    gz_send, gz_recv, gx_send, gx_recv, gc_send, gc_recv,
    sc_send, sc_recv, sx_send, sx_recv, sz_send, sz_recv, local_sem,
):
    me = lax.axis_index("vocab")
    core = lax.rem(me, NC)
    x = lax.rem(me // NC, NX)
    z = me // (NX * NC)
    vocab_rows, features = head.shape
    width = features // HALVES
    gather_width = features // GATHER_HALVES

    def index(z_, x_, c_):
        return z_ * (NX * NC) + x_ * NC + c_

    def arrival(j):
        found = jnp.int32(ARRIVALS[0][j])
        for i in range(1, NZ):
            found = jnp.where(z == i, ARRIVALS[i][j], found)
        return found

    arrived = [z] + [arrival(j) for j in range(1, NZ)]
    has_below, has_above = z > 0, z < NZ - 1
    below, above = index(z - 1, x, core), index(z + 1, x, core)

    def piece(offset):
        return pl.ds(pl.multiple_of(offset, CHUNK), CHUNK)

    def remote(source, target, send, recv, device):
        return pltpu.make_async_remote_copy(
            src_ref=source, dst_ref=target, send_sem=send, recv_sem=recv,
            device_id={"vocab": device}, device_id_type=MESH,
        )

    core_peer = index(z, x, 1 - core)
    x_peer = index(z, 1 - x, core)

    load_rows = pltpu.make_async_copy(hidden, rows.at[piece(me * CHUNK)], local_sem.at[0])
    load_head = pltpu.make_async_copy(weight, head, local_sem.at[1])
    small = [
        pltpu.make_async_copy(source, target, local_sem.at[2 + i])
        for i, (source, target) in enumerate((
            (totals, totals_row), (cotangent, cotangent_row), (labels, labels_row),
            (entry_list, list_held), (entry_valid, valid_held),
        ))
    ]
    load_rows.start()
    for copy in small:
        copy.start()
    load_head.start()

    barrier = pltpu.get_barrier_semaphore()

    def greet(peer):
        pl.semaphore_signal(barrier, inc=1, device_id={"vocab": peer}, device_id_type=MESH)

    greet(core_peer)
    greet(x_peer)
    for k in range(1, NZ):
        greet(index(lax.rem(z + k, NZ), x, core))

    load_rows.wait()
    pl.semaphore_wait(barrier, NZ + 1)

    def gather_copy(device, h, send, recv, to):
        held = rows.at[piece(device * CHUNK), h * gather_width:(h + 1) * gather_width]
        return remote(held, held, send, recv, to)

    def gather_z(j, h, to, slot):
        source = arrived[j]
        return gather_copy(
            index(source, x, core), h,
            gz_send.at[slot * GATHER_HALVES + h], gz_recv.at[source * GATHER_HALVES + h], to,
        )

    def forward_z(j, h, act):
        if j == 0:
            pl.when(has_below)(lambda: act(gather_z(0, h, below, 0)))
            pl.when(has_above)(lambda: act(gather_z(0, h, above, NZ)))
        else:
            rising = arrived[j] < z
            pl.when(rising & has_above)(lambda: act(gather_z(j, h, above, j)))
            pl.when((arrived[j] > z) & has_below)(lambda: act(gather_z(j, h, below, j)))

    def start(copy):
        copy.start()

    def sent(copy):
        copy.wait_send()

    places = [(j, h) for j in range(NZ) for h in range(GATHER_HALVES)]
    gather_x = {
        (j, h): gather_copy(
            index(arrived[j], x, core), h,
            gx_send.at[j * GATHER_HALVES + h], gx_recv.at[j * GATHER_HALVES + h], x_peer,
        )
        for j, h in places
    }
    gather_c = {
        (j, i, h): gather_copy(
            index(arrived[j], (x, 1 - x)[i], core), h,
            gc_send.at[(j * NX + i) * GATHER_HALVES + h], gc_recv.at[(j * NX + i) * GATHER_HALVES + h],
            core_peer,
        )
        for j, h in places
        for i in range(NX)
    }

    def add_logits(j, h):
        span = pl.ds(pl.multiple_of(arrived[j] * GROUP, GROUP), GROUP)
        here = slice(h * gather_width, (h + 1) * gather_width)
        for i in range(NX):
            gather_c[j, i, h].wait_recv()
        term = lax.dot_general(
            head[:, here], rows[span, here], (((1,), (1,)), ((), ())),
            preferred_element_type=jnp.float32,
        )
        if h:
            logits_acc[...] += term
        else:
            logits_acc[...] = term
        if h == GATHER_HALVES - 1:
            dlogits(j)

    def dlogits(j):
        span = pl.ds(pl.multiple_of(arrived[j] * GROUP, GROUP), GROUP)
        logits = logits_acc[...].T
        column = lax.broadcasted_iota(jnp.int32, (1, vocab_rows), 1)
        token_block = arrived[j] * GROUP // TB
        keep = jnp.zeros((1, vocab_rows), jnp.int32)
        for e in range(valid_held.shape[0]):
            used = jnp.where(
                (list_held[0, e] == token_block) & (valid_held[e] > 0), list_held[1, e], -1
            )
            keep = jnp.where(column // VB == used, 1, keep)
        hit = (labels_col[span, 0:1] == me * vocab_rows + column).astype(jnp.float32)
        value = cotangent_col[span, 0:1] * (jnp.exp(logits - totals_col[span, 0:1]) - hit)
        grad[span, :] = jnp.where(keep > 0, value, 0.0).astype(jnp.bfloat16)

    steps = [(j, h) for j in SCATTER_ORDER for h in range(HALVES)]
    scatter_c = [
        remote(core_out.at[s], core_in.at[s], sc_send.at[s], sc_recv.at[s], core_peer)
        for s in range(len(steps))
    ]
    scatter_x = [
        remote(x_out.at[s], x_in.at[s], sx_send.at[s], sx_recv.at[s], x_peer)
        for s in range(len(steps))
    ]

    def make_part(s):
        j, h = steps[s]
        span = pl.ds(pl.multiple_of(arrived[j] * GROUP, GROUP), GROUP)
        part[...] = jnp.dot(
            grad[span, :], head[:, h * width:(h + 1) * width], preferred_element_type=jnp.float32
        )
        for i in range(NX):
            here = slice(i * CHUNK, (i + 1) * CHUNK)
            core_out[s, here, :] = part[piece((i * NC + 1 - core) * CHUNK), :].astype(jnp.bfloat16)
            core_own[s, here, :] = part[piece((i * NC + core) * CHUNK), :]
        scatter_c[s].start()

    def add_core(s):
        scatter_c[s].wait_recv()
        away, own = piece((1 - x) * CHUNK), piece(x * CHUNK)
        x_out[s] = (core_own[s, away, :] + core_in[s, away, :].astype(jnp.float32)).astype(jnp.bfloat16)
        scatter_x[s].start()
        x_own[s] = core_own[s, own, :] + core_in[s, own, :].astype(jnp.float32)

    def scatter_z(s, source):
        j, h = steps[s]
        slot = source * HALVES + h
        return remote(
            z_out.at[s], z_in.at[slot], sz_send.at[s], sz_recv.at[slot],
            index(arrived[j], x, core),
        )

    def add_x(s):
        scatter_x[s].wait_recv()
        total = x_own[s] + x_in[s].astype(jnp.float32)
        if steps[s][0]:
            z_out[s] = total.astype(jnp.bfloat16)
            scatter_z(s, z).start()
        else:
            x_own[s] = total

    for h in range(GATHER_HALVES):
        gather_x[0, h].start()
        forward_z(0, h, start)
    for h in range(GATHER_HALVES):
        gather_c[0, 0, h].start()
    for copy in small:
        copy.wait()
    for vector, column in (
        (totals_row, totals_col), (cotangent_row, cotangent_col), (labels_row, labels_col)
    ):
        column[...] = jnp.broadcast_to(vector[...], (128, vector.shape[1])).T

    def pass_x(j, h):
        gather_x[j, h].wait_recv()
        gather_c[j, 1, h].start()

    waiting = []
    for j, h in places[GATHER_HALVES:]:
        gather_z(j, h, x_peer, j).wait_recv()
        forward_z(j, h, start)
        gather_x[j, h].start()
        gather_c[j, 0, h].start()
        pass_x(j - 1, h)
        if waiting:
            if len(waiting) == 1:
                load_head.wait()
            add_logits(*waiting[-1])
        waiting.append((j - 1, h))
    add_logits(*waiting[-1])
    for s in range(HALVES):
        make_part(s)
    for h in range(GATHER_HALVES):
        pass_x(NZ - 1, h)
        if h:
            add_logits(NZ - 1, h - 1)
    for s in range(HALVES):
        add_core(s)
    add_logits(NZ - 1, GATHER_HALVES - 1)

    save_rows = pltpu.make_async_copy(rows, gathered_out, local_sem.at[7])
    save_grad = pltpu.make_async_copy(grad, gradient_out, local_sem.at[8])

    passing = len(steps) - HALVES
    for s in range(HALVES, len(steps) + 3):
        if s < len(steps):
            make_part(s)
        if HALVES <= s - 1 < len(steps):
            add_core(s - 1)
        if s < 2 * HALVES:
            add_x(s - HALVES)
        if HALVES <= s - 3 < len(steps):
            add_x(s - 3)
        if s == len(steps):
            save_rows.start()
            save_grad.start()

    for h in range(HALVES):
        total = x_own[passing + h]
        for j in range(1, NZ):
            scatter_z(steps.index((j, h)), arrived[j]).wait_recv()
            total = total + z_in[arrived[j] * HALVES + h].astype(jnp.float32)
        grad_hidden[:, h * width:(h + 1) * width] = total.astype(jnp.bfloat16)

    for j, h in places:
        forward_z(j, h, sent)
    for copy in list(gather_x.values()) + list(gather_c.values()) + scatter_c + scatter_x:
        copy.wait_send()
    for s in range(passing):
        scatter_z(s, z).wait_send()
    save_rows.wait()
    save_grad.wait()


def local_fused(hidden, weight, log_totals, token_cotangent, targets, block_list, block_valid):
    tokens = log_totals.shape[0]
    vocab_rows, features = weight.shape
    entries = block_valid.shape[0]
    width = features // HALVES
    steps = NZ * HALVES
    places = NZ * GATHER_HALVES
    bf16, f32, i32 = jnp.bfloat16, jnp.float32, jnp.int32
    hbm = pl.BlockSpec(memory_space=pltpu.HBM)
    dma = pltpu.SemaphoreType.DMA
    grad_hidden, gradient, gathered = pl.pallas_call(
        head_kernel,
        out_shape=(
            jax.ShapeDtypeStruct(hidden.shape, bf16),
            jax.ShapeDtypeStruct((tokens, vocab_rows), bf16),
            jax.ShapeDtypeStruct((tokens, features), bf16),
        ),
        in_specs=[hbm] * 7,
        out_specs=(
            pl.BlockSpec(memory_space=pltpu.VMEM),
            pl.BlockSpec(memory_space=pl.ANY),
            pl.BlockSpec(memory_space=pl.ANY),
        ),
        scratch_shapes=[
            pltpu.VMEM((tokens, features), bf16),
            pltpu.VMEM((vocab_rows, features), bf16),
            pltpu.VMEM((tokens, vocab_rows), bf16),
            pltpu.VMEM((GROUP, width), f32),
            pltpu.VMEM((1, tokens), f32),
            pltpu.VMEM((1, tokens), f32),
            pltpu.VMEM((1, tokens), i32),
            pltpu.SMEM((2, entries), i32),
            pltpu.SMEM((entries,), i32),
            pltpu.VMEM((tokens, 128), f32),
            pltpu.VMEM((tokens, 128), f32),
            pltpu.VMEM((tokens, 128), i32),
            pltpu.VMEM((vocab_rows, GROUP), f32),
            pltpu.VMEM((steps, NX * CHUNK, width), bf16),
            pltpu.VMEM((steps, NX * CHUNK, width), bf16),
            pltpu.VMEM((steps, NX * CHUNK, width), f32),
            pltpu.VMEM((steps, CHUNK, width), bf16),
            pltpu.VMEM((steps, CHUNK, width), bf16),
            pltpu.VMEM((steps, CHUNK, width), f32),
            pltpu.VMEM((steps, CHUNK, width), bf16),
            pltpu.VMEM((steps, CHUNK, width), bf16),
            dma((places + GATHER_HALVES,)), dma((places,)),
            dma((places,)), dma((places,)), dma((2 * places,)), dma((2 * places,)),
            dma((steps,)), dma((steps,)), dma((steps,)), dma((steps,)),
            dma((steps,)), dma((steps,)),
            dma((9,)),
        ],
        compiler_params=pltpu.CompilerParams(
            collective_id=0, has_side_effects=True, vmem_limit_bytes=64 * 1024 * 1024
        ),
    )(
        hidden, weight, log_totals[None, :], token_cotangent[None, :], targets[None, :],
        block_list.T, block_valid,
    )
    grad_weight = lax.dot_general(
        gradient, gathered, (((0,), (0,)), ((), ())), preferred_element_type=f32
    )
    return (grad_hidden, grad_weight.astype(bf16))


def solution(mesh):
    placed = (
        P(("groups", "vocab"), None),
        P("vocab", None),
        P("groups"),
        P("groups"),
        P("groups"),
        P(("groups", "vocab"), None),
        P(("groups", "vocab")),
    )
    fused = mesh.shape["vocab"] == NZ * NX * NC
    return jax.shard_map(
        local_fused if fused else local,
        mesh=mesh,
        in_specs=placed,
        out_specs=(P(("groups", "vocab"), None), P(("groups", "vocab"), None)),
        check_vma=False,
    )
```
